32 devices in a mesh: rows: 8 (over z, x), ch: 4 (over y, core).
Axes of the slice: x: 2, y: 2, z: 4, core: 2. Of those that a mesh axis runs over, the one named last changes fastest.
Arguments:
- latent: float32 [4, 16, 160, 512], P(None, 'rows', None, 'ch'), may hold values from -12 to 12
- first_weight: float32 [27, 512, 512], P(None, 'ch'), may hold values from -0.0546875 to 0.0546875
- norm_gain: float32 [512], P('ch'), may hold values from 0.5 to 1.5
- norm_shift: float32 [512], P('ch'), may hold values from -3 to 3
- second_weight: float32 [27, 512, 256], replicated, may hold values from -0.0546875 to 0.0546875
- out_bias: float32 [256], replicated, may hold values from -3 to 3
Outputs:
- decoded: float32 [4, 32, 320, 256], P(None, ('rows', 'ch'))
The draws below stay inside these ranges and needn't reach their ends.
All inputs are finite; a program needn't handle non-finite values.
Results may differ from the reference program's by a relative error of at most 0.0001.
Values sent between devices are 32-bit elements; how exact they have to be, the bound alone decides.
A program may use at most 320 MiB of HBM per device.

```python
import math
import jax
import jax.numpy as jnp
from jax import lax

C1 = 512
C2 = 256
GROUPS = 32
FRAMES = 4
COLS = 160
ROWS_ALL = 16


def draw_latent(key, part):
    keys = jax.random.split(jax.random.fold_in(key, 11), 3)
    positions = jnp.arange(ROWS_ALL, dtype=jnp.float32)
    row_scale = jnp.exp(math.log(3.0) * positions / max(ROWS_ALL - 1, 1)) * jax.random.uniform(keys[0], (ROWS_ALL,), jnp.float32, 0.7, 1.4)
    chan_scale = jnp.exp(jax.random.uniform(keys[1], (C1,), jnp.float32, math.log(0.3), math.log(3.0)))
    shape = (FRAMES, ROWS_ALL, COLS, C1)
    base = jax.random.normal(keys[2], shape, jnp.float32)
    values = base * row_scale[None, :, None, None] * chan_scale
    return jnp.clip(values, -12.0, 12.0)


def shard_levels(stream_key, dims, pieces, smallest, top_value):
    loudness = 1.0
    for dim, shards_of in pieces:
        draws = jax.random.uniform(jax.random.fold_in(jax.random.fold_in(stream_key, 6), dim), (shards_of,), jnp.float32, smallest / len(pieces), top_value / len(pieces))
        loudness = loudness * jnp.repeat(jnp.exp(draws), dims[dim] // shards_of).reshape((-1,) + (1,) * (len(dims) - 1 - dim))
    return loudness


def normal_values(key, extent, deviation, most, cuts=(), held_as=jnp.bfloat16):
    drawn = jax.random.normal(key, extent, jnp.float32) * deviation
    if len(cuts) > 0:
        drawn = shard_levels(key, extent, cuts, -0.22, 0.18) * drawn
    return jnp.clip(drawn, min=-most, max=most).astype(held_as)


def setup_inputs(seed: int = 0) -> dict:
    splits = jax.random.split(jax.random.key(seed), 7)
    latent = draw_latent(jax.random.fold_in(splits[6], 71), 0)
    first_weight = normal_values(splits[1], (27, C1, C1), (27 * C1) ** -0.5, 0.0546875, ((1, 4),), jnp.float32)
    norm_gain = jnp.clip(1.0 + 0.1 * jax.random.normal(splits[2], (C1,), jnp.float32), 0.5, 1.5)
    norm_shift = normal_values(splits[3], (C1,), 0.5, 3.0, ((0, 4),), jnp.float32)
    second_weight = normal_values(splits[4], (27, C1, C2), (27 * C1) ** -0.5, 0.0546875, (), jnp.float32)
    out_bias = normal_values(splits[5], (C2,), 0.5, 3.0, (), jnp.float32)
    return {"latent": latent, "first_weight": first_weight, "norm_gain": norm_gain, "norm_shift": norm_shift, "second_weight": second_weight, "out_bias": out_bias}


epsilon = 1e-06

def pad_edges(field):
    first_frame = field[:1]
    field = jnp.concatenate([first_frame, first_frame, field], axis=0)
    return jnp.pad(field, ((0, 0), (0, 0), (1, 1), (0, 0)))

def convolve(padded, weights, frames, height, breadth):
    inner = padded.shape[-1]
    total = jnp.zeros((frames * height * breadth, weights.shape[-1]), jnp.float32)
    for time_tap in range(3):
        for row_tap in range(3):
            for col_tap in range(3):
                piece = padded[time_tap:time_tap + frames, row_tap:row_tap + height, col_tap:col_tap + breadth, :]
                total = total + jnp.dot(piece.reshape(-1, inner), weights[9 * time_tap + 3 * row_tap + col_tap], precision=lax.Precision.HIGHEST, preferred_element_type=jnp.float32)
    return total.reshape(frames, height, breadth, -1)

def causal_conv(field, weights):
    frames, height, breadth, inner = field.shape
    rimmed = jnp.pad(field, ((0, 0), (1, 1), (0, 0), (0, 0)))
    return convolve(pad_edges(rimmed), weights, frames, height, breadth)

def reference(latent, first_weight, norm_gain, norm_shift, second_weight, out_bias):
    frames, height, breadth, width = latent.shape
    first = causal_conv(latent, first_weight)
    grouped = first.reshape(frames, height, breadth, GROUPS, width // GROUPS)
    mean = lax.optimization_barrier(jnp.mean(grouped, axis=(0, 1, 2, 4), keepdims=True))
    centered = grouped - mean
    variance = lax.optimization_barrier(jnp.mean(centered * centered, axis=(0, 1, 2, 4), keepdims=True))
    normed = (centered / jnp.sqrt(variance + epsilon)).reshape(frames, height, breadth, width)
    hidden = jax.nn.silu(normed * norm_gain + norm_shift)
    upsampled = jnp.repeat(jnp.repeat(hidden, 2, axis=1), 2, axis=2)
    return causal_conv(upsampled, second_weight) + out_bias
```

```python
import functools

import jax
import jax.numpy as jnp
from jax import lax
from jax.experimental import pallas as pl
from jax.experimental.pallas import tpu as pltpu
from jax.sharding import PartitionSpec as P

GROUPS = 32
epsilon = 1e-06
VMEM_LIMIT = 56 * 1024 * 1024


def split(value):
    high = value.astype(jnp.bfloat16)
    low = (value - high.astype(jnp.float32)).astype(jnp.bfloat16)
    return high, low


def shifted(value):
    count = value.shape[0]
    place = lax.broadcasted_iota(jnp.int32, value.shape, 0)
    left = jnp.where(place == 0, 0.0, pltpu.roll(value, 1, 0))
    right = jnp.where(place == count - 1, 0.0, pltpu.roll(value, count - 1, 0))
    return left, value, right


def dot(a, b):
    return jnp.dot(a, b, preferred_element_type=jnp.float32)


def first_kernel(x_ref, w_ref, out_ref, xc_ref):
    frames, height, breadth, outer = out_ref.shape
    inner = x_ref.shape[-1]
    step = pl.program_id(0)

    @pl.when(step == 0)
    def _():
        for frame in range(frames):
            for row in range(height + 2):
                for k, piece in enumerate(shifted(x_ref[frame, row])):
                    high, low = split(piece)
                    for target in (0, 1, 2) if frame == 0 else (frame + 2,):
                        xc_ref[target, row, :, k * inner:(k + 1) * inner] = high
                        xc_ref[target, row, :, (3 + k) * inner:(4 + k) * inner] = low
        out_ref[...] = jnp.zeros_like(out_ref)

    high, low = split(w_ref[...].reshape(3 * inner, outer))
    both = jnp.concatenate([high, high], axis=0)
    slab = xc_ref[pl.ds(step // 3, frames), pl.ds(step % 3, height)]
    slab = slab.reshape(frames * height * breadth, 6 * inner)
    term = dot(slab, both) + dot(slab[:, :3 * inner], low)
    out_ref[...] += term.reshape(out_ref.shape)


def first_conv(x, weights):
    frames, rows, breadth, inner = x.shape
    outer = weights.shape[-1]
    shape = (frames, rows - 2, breadth, outer)
    return pl.pallas_call(
        first_kernel,
        grid=(9,),
        in_specs=[
            pl.BlockSpec(x.shape, lambda i: (0, 0, 0, 0)),
            pl.BlockSpec((3, inner, outer), lambda i: (i, 0, 0)),
        ],
        out_specs=pl.BlockSpec(shape, lambda i: (0, 0, 0, 0)),
        out_shape=jax.ShapeDtypeStruct(shape, jnp.float32),
        scratch_shapes=[pltpu.VMEM((frames + 2, rows, breadth, 6 * inner), jnp.bfloat16)],
        compiler_params=pltpu.CompilerParams(vmem_limit_bytes=VMEM_LIMIT),
    )(x, weights)


def second_kernel(phase_ref, h_ref, w_ref, b_ref, out_ref, xc_ref, acc_ref, mix_ref):
    frames, _, breadth, _ = h_ref.shape
    lanes = out_ref.shape[3] // 128
    part = w_ref.shape[1]
    parts = h_ref.shape[3] // part
    step = pl.program_id(0)
    half = step % parts

    @pl.when(step == 0)
    def _():
        for p in range(parts):
            for frame in range(frames):
                for row in range(2):
                    value = h_ref[frame, row, :, p * part:(p + 1) * part]
                    for k, piece in enumerate(shifted(value)):
                        high, low = split(piece)
                        for target in (0, 1, 2) if frame == 0 else (frame + 2,):
                            xc_ref[p, target, row, :, k * part:(k + 1) * part] = high
                            xc_ref[p, target, row, :, (3 + k) * part:(4 + k) * part] = low
        acc_ref[...] = jnp.zeros_like(acc_ref)

    odd = phase_ref[0:1, 0:1]
    for row in range(2):
        taps = []
        for col in range(3):
            middle = w_ref[3 + col]
            if row == 0:
                taps.append(w_ref[col] + odd * middle)
            else:
                taps.append(w_ref[6 + col] + (1.0 - odd) * middle)
        slab = xc_ref[half, pl.ds(step // parts, frames), row]
        slab = slab.reshape(frames * breadth, 6 * part)
        for q in range(2):
            pair = [taps[0], taps[1] + taps[2]] if q == 0 else [taps[0] + taps[1], taps[2]]
            high, low = split(jnp.concatenate(pair, axis=0))
            x_high = slab[:, q * part:(q + 2) * part]
            x_low = slab[:, (3 + q) * part:(5 + q) * part]
            acc_ref[q] += dot(x_high, high) + dot(x_low, high) + dot(x_high, low)

    @pl.when(step == pl.num_programs(0) - 1)
    def _():
        for frame in range(frames):
            for q in range(2):
                rows = acc_ref[q, frame * breadth:(frame + 1) * breadth, :] + b_ref[...]
                for lane in range(lanes):
                    mix_ref[lane, pl.ds(q, breadth, stride=2), :] = rows[:, lane * 128:(lane + 1) * 128]
            for lane in range(lanes):
                out_ref[frame, 0, :, lane * 128:(lane + 1) * 128] = mix_ref[lane]


def second_conv(phase, hidden, weights, bias):
    frames, _, breadth, inner = hidden.shape
    outer = weights.shape[-1]
    part = inner // 2
    shape = (frames, 1, 2 * breadth, outer)
    return pl.pallas_call(
        second_kernel,
        grid=(6,),
        in_specs=[
            pl.BlockSpec(phase.shape, lambda i: (0, 0)),
            pl.BlockSpec(hidden.shape, lambda i: (0, 0, 0, 0)),
            pl.BlockSpec((9, part, outer), lambda i: (i // 2, i % 2, 0)),
            pl.BlockSpec((1, outer), lambda i: (0, 0)),
        ],
        out_specs=pl.BlockSpec(shape, lambda i: (0, 0, 0, 0)),
        out_shape=jax.ShapeDtypeStruct(shape, jnp.float32),
        scratch_shapes=[
            pltpu.VMEM((2, frames + 2, 2, breadth, 6 * part), jnp.bfloat16),
            pltpu.VMEM((2, frames * breadth, outer), jnp.float32),
            pltpu.VMEM((outer // 128, 2 * breadth, 128), jnp.float32),
        ],
        compiler_params=pltpu.CompilerParams(vmem_limit_bytes=VMEM_LIMIT),
    )(phase, hidden, weights, bias.reshape(1, outer))


def with_halo(cells, axis, dim):
    count = lax.axis_size(axis)
    ends = count - 1
    head = lax.slice_in_dim(cells, 0, 1, axis=dim)
    tail = lax.slice_in_dim(cells, cells.shape[dim] - 1, cells.shape[dim], axis=dim)
    return jnp.concatenate(
        [
            lax.ppermute(tail, axis, [(i, i + 1) for i in range(ends)]),
            cells,
            lax.ppermute(head, axis, [(i + 1, i) for i in range(ends)]),
        ],
        axis=dim,
    )


def shards(latent, first_weight, norm_gain, norm_shift, second_weight, out_bias):
    frames, height, breadth, inner = latent.shape
    channels = first_weight.shape[-1]
    partial_value = first_conv(with_halo(latent, "rows", 1), first_weight)
    first = lax.psum_scatter(partial_value, "ch", scatter_dimension=3, tiled=True)
    local_width = first.shape[3]
    group_width = channels // GROUPS
    groups_here = local_width // group_width
    count = float(frames * height * lax.axis_size("rows") * breadth * group_width)
    sums = jnp.stack([jnp.sum(first, axis=(0, 1, 2)), jnp.sum(first * first, axis=(0, 1, 2))])
    sums = lax.psum(sums.reshape(2, groups_here, group_width).sum(-1), "rows") / count
    mean = sums[0]
    variance = sums[1] - mean * mean
    gain = jnp.repeat(1.0 / jnp.sqrt(variance + epsilon), group_width) * norm_gain
    hidden = jax.nn.silu((first - jnp.repeat(mean, group_width)) * gain + norm_shift)
    ext = lax.all_gather(with_halo(hidden, "rows", 1), "ch", axis=3, tiled=True)
    place = lax.axis_index("ch")
    mine = lax.dynamic_slice_in_dim(ext, (place + 1) // 2, 2, 1)
    phase = jnp.full((8, 128), place % 2, jnp.float32)
    return second_conv(phase, mine, second_weight, out_bias)


def solution(mesh):
    return jax.shard_map(
        shards,
        mesh=mesh,
        in_specs=(P(None, "rows", None, "ch"), P(None, "ch", None), P("ch"), P("ch"), P(), P()),
        out_specs=P(None, ("rows", "ch"), None, None),
        check_vma=False,
    )
```

```python
import functools

import jax
import jax.numpy as jnp
from jax import lax
from jax.experimental import pallas as pl
from jax.experimental.pallas import tpu as pltpu
from jax.sharding import PartitionSpec as P

GROUPS = 32
epsilon = 1e-06
VMEM_LIMIT = 58 * 1024 * 1024


def split(value):
    high = value.astype(jnp.bfloat16)
    low = (value - high.astype(jnp.float32)).astype(jnp.bfloat16)
    return high, low


def shifted(value):
    count = value.shape[0]
    place = lax.broadcasted_iota(jnp.int32, value.shape, 0)
    left = jnp.where(place == 0, 0.0, pltpu.roll(value, 1, 0))
    right = jnp.where(place == count - 1, 0.0, pltpu.roll(value, count - 1, 0))
    return left, value, right


def dot(a, b):
    return jnp.dot(a, b, preferred_element_type=jnp.float32)


def store_shifted(target_ref, frame, row, value):
    width = value.shape[-1]
    for k, piece in enumerate(shifted(value)):
        high, low = split(piece)
        for place in (0, 1, 2) if frame == 0 else (frame + 2,):
            target_ref[place, row, :, k * width:(k + 1) * width] = high
            target_ref[place, row, :, (3 + k) * width:(4 + k) * width] = low


def remote(src, dst, send, recv, rows, ch):
    return pltpu.make_async_remote_copy(
        src_ref=src, dst_ref=dst, send_sem=send, recv_sem=recv,
        device_id={"rows": rows, "ch": ch}, device_id_type=pl.DeviceIdType.MESH,
    )


def block_kernel(
    ring, count,
    x_ref, gain_ref, shift_ref, bias_ref, w1_hbm, w2_hbm,
    out_ref,
    stage_ref, high_ref, low_ref, halo_ref, xc1_ref, acc1_ref, part_ref, partin_ref,
    sum_ref, sumin_ref, raw_ref, stats_ref, vec_ref, gs_ref, w2_ref, xc2_ref, acc2_ref, mix_ref,
    w1_sem, w2_sem, halo_send, halo_recv, gs_send, gs_recv, part_send, part_recv,
    sum_send, sum_recv, stats_send, stats_recv, gather_send, gather_recv,
    row_send, row_recv, vec_send, vec_recv,
):
    frames, height, breadth, inner = x_ref.shape
    half_width = raw_ref.shape[-1]
    r = lax.axis_index("rows")
    c = lax.axis_index("ch")
    u = lax.rem(c, 2)
    v = lax.div(c, 2)
    pair = c + 1 - 2 * u
    across = c + 2 - 4 * v
    other = 1 - v
    peers = 2 * ring

    for t in range(3):
        pltpu.make_async_copy(w1_hbm.at[pl.ds(9 * t, 9)], stage_ref.at[pl.ds(9 * t, 9)], w1_sem.at[t]).start()

    def w2_copy(i):
        half = v if i < 3 else other
        start = pl.multiple_of(half * half_width, half_width)
        return pltpu.make_async_copy(
            w2_hbm.at[pl.ds(9 * (i % 3), 9), pl.ds(start, half_width)], w2_ref.at[i % 2], w2_sem.at[i % 2]
        )

    w2_copy(0).start()
    w2_copy(1).start()

    barrier = pltpu.get_barrier_semaphore()

    def greet(rows, ch):
        pl.semaphore_signal(
            barrier, inc=1, device_id={"rows": rows, "ch": ch}, device_id_type=pl.DeviceIdType.MESH
        )

    @pl.loop(0, ring)
    def _(i):
        greet(i, pair)

        @pl.when(i != r)
        def _():
            greet(i, c)

    greet(r, across)
    pl.semaphore_wait(barrier, peers)

    up, down = r > 0, r < ring - 1
    halo_down = remote(x_ref.at[:, pl.ds(height - 1, 1)], halo_ref.at[0], halo_send.at[0], halo_recv.at[0], r + 1, c)
    halo_up = remote(x_ref.at[:, pl.ds(0, 1)], halo_ref.at[1], halo_send.at[1], halo_recv.at[1], r - 1, c)
    pl.when(down)(halo_down.start)
    pl.when(up)(halo_up.start)

    gs_ref[u] = jnp.zeros(gs_ref.shape[1:], jnp.float32)
    gs_ref[u, 0:1, :] = gain_ref[...]
    gs_ref[u, 1:2, :] = shift_ref[...]
    gs_copy = remote(gs_ref.at[u], gs_ref.at[u], gs_send, gs_recv, r, pair)
    gs_copy.start()

    for frame in range(frames):
        for row in range(height):
            store_shifted(xc1_ref, frame, row + 1, x_ref[frame, row])

    for t in range(3):
        pltpu.make_async_copy(w1_hbm.at[pl.ds(9 * t, 9)], stage_ref.at[pl.ds(9 * t, 9)], w1_sem.at[t]).wait()

        @pl.loop(3 * t, 3 * t + 3)
        def _(g):
            high, low = split(stage_ref[pl.ds(3 * g, 3)].reshape(3 * inner, 2 * half_width))
            for n in range(2):
                high_ref[n, g] = high[:, n * half_width:(n + 1) * half_width]
                low_ref[n, g] = low[:, n * half_width:(n + 1) * half_width]

    def first_step(row, n, t, tap):
        slab = xc1_ref[pl.ds(t, frames), pl.ds(row + tap, 1)].reshape(frames * breadth, 6 * inner)
        high = high_ref[n, 3 * t + tap]
        low = low_ref[n, 3 * t + tap]
        both = jnp.concatenate([high, high], axis=0)
        acc1_ref[...] += dot(slab, both) + dot(slab[:, :3 * inner], low)

    def inner_taps(row, n):
        acc1_ref[...] = jnp.zeros_like(acc1_ref)

        @pl.loop(0, 6)
        def _(i):
            first_step(row, n, lax.div(i, 2), 1 - row + lax.rem(i, 2))

    def outer_taps(row, n):
        @pl.loop(0, 3)
        def _(i):
            first_step(row, n, i, 2 * row)

    inner_taps(1 - u, other)

    @pl.when(up)
    def _():
        halo_down.wait_recv()

    @pl.when(down)
    def _():
        halo_up.wait_recv()

    @pl.when(r == 0)
    def _():
        halo_ref[0] = jnp.zeros(halo_ref.shape[1:], jnp.float32)

    @pl.when(r == ring - 1)
    def _():
        halo_ref[1] = jnp.zeros(halo_ref.shape[1:], jnp.float32)

    for frame in range(frames):
        store_shifted(xc1_ref, frame, 0, halo_ref[0, frame, 0])
        store_shifted(xc1_ref, frame, height + 1, halo_ref[1, frame, 0])
    outer_taps(1 - u, other)
    part_copies = [
        remote(part_ref.at[i], partin_ref.at[i], part_send.at[i], part_recv.at[i], r, pair) for i in range(2)
    ]
    part_ref[0] = acc1_ref[...]
    part_copies[0].start()

    inner_taps(u, other)
    outer_taps(u, other)
    part_copies[0].wait_recv()
    sum_ref[...] = acc1_ref[...] + partin_ref[0]
    sum_copy = remote(sum_ref, sumin_ref, sum_send, sum_recv, r, across)
    sum_copy.start()

    inner_taps(1 - u, v)
    outer_taps(1 - u, v)
    part_ref[1] = acc1_ref[...]
    part_copies[1].start()

    inner_taps(u, v)
    outer_taps(u, v)
    part_copies[1].wait_recv()
    acc1_ref[...] += partin_ref[1]
    sum_copy.wait_recv()
    mine = acc1_ref[...] + sumin_ref[...]
    raw_ref[other, v] = mine

    user = r + jnp.where(c == 1, 1, 0) - jnp.where(c == 2, 1, 0)
    source = r - jnp.where(c == 0, 1, 0) + jnp.where(c == 3, 1, 0)
    used = jnp.logical_and(user >= 0, user < ring)
    fed = jnp.logical_and(source >= 0, source < ring)
    gather = remote(raw_ref.at[other, v], raw_ref.at[v, v], gather_send, gather_recv, r, across)
    gather.start()
    row_copies = [
        remote(raw_ref.at[other, h], raw_ref.at[v, h], row_send.at[i], row_recv.at[i], user, pair)
        for i, h in enumerate((v, other))
    ]
    pl.when(used)(row_copies[0].start)

    slot = 2 * r + u
    stats_ref[slot] = jnp.zeros(stats_ref.shape[1:], jnp.float32)
    stats_ref[slot, 0:1, :] = jnp.sum(mine, axis=0, keepdims=True)
    stats_ref[slot, 1:2, :] = jnp.sum(mine * mine, axis=0, keepdims=True)

    def stats_copy(i):
        return remote(
            stats_ref.at[slot], stats_ref.at[slot], stats_send.at[i], stats_recv.at[slot],
            lax.div(i, 2), 2 * v + lax.rem(i, 2),
        )

    def stats_arrival(i):
        return remote(
            stats_ref.at[i], stats_ref.at[i], stats_send.at[i], stats_recv.at[i],
            lax.div(i, 2), 2 * v + lax.rem(i, 2),
        )

    @pl.loop(0, peers)
    def _(i):
        @pl.when(i != slot)
        def _():
            stats_copy(i).start()

    @pl.loop(0, peers)
    def _(i):
        @pl.when(i != slot)
        def _():
            stats_arrival(i).wait_recv()

    sums = jnp.sum(stats_ref[:, 0:2, :], axis=0)
    group = 2 * half_width // GROUPS
    line = lax.div(lax.broadcasted_iota(jnp.int32, (half_width, half_width), 0), group)
    column = lax.div(lax.broadcasted_iota(jnp.int32, (half_width, half_width), 1), group)
    members = (line == column).astype(jnp.float32)
    eight = jnp.concatenate([sums, jnp.zeros((6, half_width), jnp.float32)], axis=0)
    totals = jnp.dot(eight, members, precision=lax.Precision.HIGHEST, preferred_element_type=jnp.float32)
    mean = totals[0:1] / count
    variance = totals[1:2] / count - mean * mean
    gs_copy.wait_recv()
    gain = jnp.concatenate([gs_ref[0, 0:1, :], gs_ref[1, 0:1, :]], axis=1)
    vec_ref[v] = jnp.zeros(vec_ref.shape[1:], jnp.float32)
    vec_ref[v, 0:1, :] = mean
    vec_ref[v, 1:2, :] = gain / jnp.sqrt(variance + epsilon)
    vec_ref[v, 2:3, :] = jnp.concatenate([gs_ref[0, 1:2, :], gs_ref[1, 1:2, :]], axis=1)
    vec_copy = remote(vec_ref.at[v], vec_ref.at[v], vec_send, vec_recv, r, across)
    vec_copy.start()

    acc2_ref[...] = jnp.zeros_like(acc2_ref)
    odd = u.astype(jnp.float32)

    @pl.when(jnp.logical_not(fed))
    def _():
        raw_ref[v] = jnp.zeros(raw_ref.shape[1:], jnp.float32)

    def normalise(half):
        mean, scale, shift = (vec_ref[half, i:i + 1, :] for i in range(3))
        for row in range(2):
            keep = jnp.where(jnp.logical_or(fed, row != v), 1.0, 0.0)
            for frame in range(frames):
                value = raw_ref[row, half, frame * breadth:(frame + 1) * breadth, :]
                value = (value - mean) * scale + shift
                value = value / (1.0 + jnp.exp(-value))
                store_shifted(xc2_ref, frame, row, value * keep)

    def second_step(i):
        w2_copy(i).wait()
        w_ref = w2_ref.at[i % 2]
        t = i % 3
        for row in range(2):
            taps = []
            for col in range(3):
                middle = w_ref[3 + col]
                if row == 0:
                    taps.append(w_ref[col] + odd * middle)
                else:
                    taps.append(w_ref[6 + col] + (1.0 - odd) * middle)
            slab = xc2_ref[t:t + frames, row].reshape(frames * breadth, 6 * half_width)
            for q in range(2):
                both = [taps[0], taps[1] + taps[2]] if q == 0 else [taps[0] + taps[1], taps[2]]
                high, low = split(jnp.concatenate(both, axis=0))
                x_high = slab[:, q * half_width:(q + 2) * half_width]
                x_low = slab[:, (3 + q) * half_width:(5 + q) * half_width]
                acc2_ref[q] += dot(x_high, high) + dot(x_low, high) + dot(x_high, low)
        if i + 2 < 6:
            w2_copy(i + 2).start()

    pl.when(fed)(row_copies[0].wait_recv)
    normalise(v)
    for i in range(3):
        second_step(i)

    gather.wait_recv()
    pl.when(used)(row_copies[1].start)
    vec_copy.wait_recv()
    pl.when(fed)(row_copies[1].wait_recv)
    normalise(other)
    for i in range(3, 6):
        second_step(i)

    lanes = out_ref.shape[3] // 128
    for frame in range(frames):
        for q in range(2):
            rows = acc2_ref[q, frame * breadth:(frame + 1) * breadth, :] + bias_ref[...]
            for lane in range(lanes):
                mix_ref[lane, pl.ds(q, breadth, stride=2), :] = rows[:, lane * 128:(lane + 1) * 128]
        for lane in range(lanes):
            out_ref[frame, 0, :, lane * 128:(lane + 1) * 128] = mix_ref[lane]

    pl.when(down)(halo_down.wait_send)
    pl.when(up)(halo_up.wait_send)
    gs_copy.wait_send()
    part_copies[0].wait_send()
    part_copies[1].wait_send()
    sum_copy.wait_send()
    gather.wait_send()
    vec_copy.wait_send()

    @pl.when(used)
    def _():
        row_copies[0].wait_send()
        row_copies[1].wait_send()

    @pl.loop(0, peers)
    def _(i):
        @pl.when(i != slot)
        def _():
            stats_copy(i).wait_send()


def shards(latent, first_weight, norm_gain, norm_shift, second_weight, out_bias):
    frames, height, breadth, inner = latent.shape
    channels = first_weight.shape[-1]
    outer = second_weight.shape[-1]
    ring = lax.axis_size("rows")
    half = channels // 2
    pixels = frames * breadth
    count = float(frames * height * ring * breadth * (channels // GROUPS))
    f32, b16 = jnp.float32, jnp.bfloat16
    dma = pltpu.SemaphoreType.DMA
    vmem = pl.BlockSpec(memory_space=pltpu.VMEM)
    hbm = pl.BlockSpec(memory_space=pl.ANY)
    return pl.pallas_call(
        functools.partial(block_kernel, ring, count),
        out_shape=jax.ShapeDtypeStruct((frames, 1, 2 * breadth, outer), f32),
        in_specs=[vmem, vmem, vmem, vmem, hbm, hbm],
        out_specs=vmem,
        scratch_shapes=[
            pltpu.VMEM(first_weight.shape, f32),
            pltpu.VMEM((2, 9, 3 * inner, half), b16),
            pltpu.VMEM((2, 9, 3 * inner, half), b16),
            pltpu.VMEM((2, frames, 1, breadth, inner), f32),
            pltpu.VMEM((frames + 2, height + 2, breadth, 6 * inner), b16),
            pltpu.VMEM((pixels, half), f32),
            pltpu.VMEM((2, pixels, half), f32),
            pltpu.VMEM((2, pixels, half), f32),
            pltpu.VMEM((pixels, half), f32),
            pltpu.VMEM((pixels, half), f32),
            pltpu.VMEM((2, 2, pixels, half), f32),
            pltpu.VMEM((2 * ring, 8, half), f32),
            pltpu.VMEM((2, 8, half), f32),
            pltpu.VMEM((2, 8, inner), f32),
            pltpu.VMEM((2, 9, half, outer), f32),
            pltpu.VMEM((frames + 2, 2, breadth, 6 * half), b16),
            pltpu.VMEM((2, pixels, outer), f32),
            pltpu.VMEM((outer // 128, 2 * breadth, 128), f32),
            dma((3,)), dma((2,)), dma((2,)), dma((2,)), dma, dma, dma((2,)), dma((2,)),
            dma, dma, dma((2 * ring,)), dma((2 * ring,)), dma, dma,
            dma((2,)), dma((2,)), dma, dma,
        ],
        compiler_params=pltpu.CompilerParams(
            collective_id=0, has_side_effects=True, vmem_limit_bytes=VMEM_LIMIT
        ),
    )(
        latent, norm_gain.reshape(1, inner), norm_shift.reshape(1, inner), out_bias.reshape(1, outer),
        first_weight, second_weight,
    )


def solution(mesh):
    return jax.shard_map(
        shards,
        mesh=mesh,
        in_specs=(P(None, "rows", None, "ch"), P(None, "ch", None), P("ch"), P("ch"), P(), P()),
        out_specs=P(None, ("rows", "ch"), None, None),
        check_vma=False,
    )
```

```python
import functools

import jax
import jax.numpy as jnp
from jax import lax
from jax.experimental import pallas as pl
from jax.experimental.pallas import tpu as pltpu
from jax.sharding import PartitionSpec as P

GROUPS = 32
epsilon = 1e-06
VMEM_LIMIT = 58 * 1024 * 1024


def split(value):
    high = value.astype(jnp.bfloat16)
    low = (value - high.astype(jnp.float32)).astype(jnp.bfloat16)
    return high, low


def shifted(value):
    count = value.shape[0]
    place = lax.broadcasted_iota(jnp.int32, value.shape, 0)
    left = jnp.where(place == 0, 0.0, pltpu.roll(value, 1, 0))
    right = jnp.where(place == count - 1, 0.0, pltpu.roll(value, count - 1, 0))
    return left, value, right


def dot(a, b):
    return jnp.dot(a, b, preferred_element_type=jnp.float32)


def store_shifted(target_ref, frame, row, value):
    width = value.shape[-1]
    for k, piece in enumerate(shifted(value)):
        high, low = split(piece)
        for place in (0, 1, 2) if frame == 0 else (frame + 2,):
            target_ref[place, row, :, k * width:(k + 1) * width] = high
            target_ref[place, row, :, (3 + k) * width:(4 + k) * width] = low


def remote(src, dst, send, recv, rows, ch):
    return pltpu.make_async_remote_copy(
        src_ref=src, dst_ref=dst, send_sem=send, recv_sem=recv,
        device_id={"rows": rows, "ch": ch}, device_id_type=pl.DeviceIdType.MESH,
    )


def block_kernel(
    ring, count,
    x_ref, gain_ref, shift_ref, bias_ref, w1_hbm, w2_hbm,
    out_ref,
    stage_ref, high_ref, low_ref, halo_ref, xc1_ref, acc1_ref, part_ref, partin_ref,
    sum_ref, sumin_ref, raw_ref, stats_ref, vec_ref, gs_ref, w2_ref, xc2_ref, acc2_ref, mix_ref,
    w1_sem, w2_sem, halo_send, halo_recv, gs_send, gs_recv, part_send, part_recv,
    sum_send, sum_recv, stats_send, stats_recv, gather_send, gather_recv,
    row_send, row_recv, vec_send, vec_recv,
):
    frames, height, breadth, inner = x_ref.shape
    half_width = raw_ref.shape[-1]
    r = lax.axis_index("rows")
    c = lax.axis_index("ch")
    u = lax.rem(c, 2)
    v = lax.div(c, 2)
    pair = c + 1 - 2 * u
    across = c + 2 - 4 * v
    other = 1 - v
    peers = 2 * ring

    for t in range(3):
        pltpu.make_async_copy(w1_hbm.at[pl.ds(9 * t, 9)], stage_ref.at[pl.ds(9 * t, 9)], w1_sem.at[t]).start()

    def w2_copy(i):
        half = v if i < 3 else other
        start = pl.multiple_of(half * half_width, half_width)
        return pltpu.make_async_copy(
            w2_hbm.at[pl.ds(9 * (i % 3), 9), pl.ds(start, half_width)], w2_ref.at[i % 2], w2_sem.at[i % 2]
        )

    w2_copy(0).start()
    w2_copy(1).start()

    barrier = pltpu.get_barrier_semaphore()

    def greet(rows, ch):
        pl.semaphore_signal(
            barrier, inc=1, device_id={"rows": rows, "ch": ch}, device_id_type=pl.DeviceIdType.MESH
        )

    @pl.loop(0, ring)
    def _(i):
        greet(i, pair)

        @pl.when(i != r)
        def _():
            greet(i, c)

    greet(r, across)
    pl.semaphore_wait(barrier, peers)

    up, down = r > 0, r < ring - 1
    parts = 2
    some = frames // parts
    span = some * breadth
    halo_down, halo_up = [], []
    for p in range(parts):
        when = pl.ds(p * some, some)
        halo_down.append(remote(
            x_ref.at[when, pl.ds(height - 1, 1)], halo_ref.at[0, when], halo_send.at[p], halo_recv.at[p], r + 1, c
        ))
        halo_up.append(remote(
            x_ref.at[when, pl.ds(0, 1)], halo_ref.at[1, when],
            halo_send.at[parts + p], halo_recv.at[parts + p], r - 1, c,
        ))
        pl.when(down)(halo_down[p].start)
        pl.when(up)(halo_up[p].start)

    gs_ref[u] = jnp.zeros(gs_ref.shape[1:], jnp.float32)
    gs_ref[u, 0:1, :] = gain_ref[...]
    gs_ref[u, 1:2, :] = shift_ref[...]
    gs_copy = remote(gs_ref.at[u], gs_ref.at[u], gs_send, gs_recv, r, pair)
    gs_copy.start()

    for frame in range(frames):
        for row in range(height):
            store_shifted(xc1_ref, frame, row + 1, x_ref[frame, row])

    for t in range(3):
        pltpu.make_async_copy(w1_hbm.at[pl.ds(9 * t, 9)], stage_ref.at[pl.ds(9 * t, 9)], w1_sem.at[t]).wait()

        @pl.loop(3 * t, 3 * t + 3)
        def _(g):
            high, low = split(stage_ref[pl.ds(3 * g, 3)].reshape(3 * inner, 2 * half_width))
            for n in range(2):
                high_ref[n, g] = high[:, n * half_width:(n + 1) * half_width]
                low_ref[n, g] = low[:, n * half_width:(n + 1) * half_width]

    def first_step(acc, row, n, t, tap, begin, length):
        slab = xc1_ref[pl.ds(t + begin, length), pl.ds(row + tap, 1)].reshape(length * breadth, 6 * inner)
        high = high_ref[n, 3 * t + tap]
        low = low_ref[n, 3 * t + tap]
        both = jnp.concatenate([high, high], axis=0)
        acc[pl.ds(begin * breadth, length * breadth), :] += dot(slab, both) + dot(slab[:, :3 * inner], low)

    def inner_taps(acc, row, n):
        acc[...] = jnp.zeros(acc.shape, jnp.float32)

        @pl.loop(0, 6)
        def _(i):
            first_step(acc, row, n, lax.div(i, 2), 1 - row + lax.rem(i, 2), 0, frames)

    def outer_taps(acc, row, n, begin=0, length=frames):
        @pl.loop(0, 3)
        def _(i):
            first_step(acc, row, n, i, 2 * row, begin, length)

    sent = [part_ref.at[0], part_ref.at[1]]
    inner_taps(sent[0], 1 - u, other)
    inner_taps(acc1_ref, u, other)

    @pl.when(r == 0)
    def _():
        halo_ref[0] = jnp.zeros(halo_ref.shape[1:], jnp.float32)

    @pl.when(r == ring - 1)
    def _():
        halo_ref[1] = jnp.zeros(halo_ref.shape[1:], jnp.float32)

    part_copies, sum_copies = [], []
    for p in range(parts):
        pl.when(up)(halo_down[p].wait_recv)
        pl.when(down)(halo_up[p].wait_recv)
        for frame in range(p * some, (p + 1) * some):
            store_shifted(xc1_ref, frame, 0, halo_ref[0, frame, 0])
            store_shifted(xc1_ref, frame, height + 1, halo_ref[1, frame, 0])
        where = pl.ds(p * span, span)
        outer_taps(sent[0], 1 - u, other, p * some, some)
        part_copies.append(remote(
            part_ref.at[0, where], partin_ref.at[0, where], part_send.at[p], part_recv.at[p], r, pair
        ))
        part_copies[p].start()
        outer_taps(acc1_ref, u, other, p * some, some)
        part_copies[p].wait_recv()
        sum_ref[where, :] = acc1_ref[where, :] + partin_ref[0, where, :]
        sum_copies.append(remote(
            sum_ref.at[where], sumin_ref.at[where], sum_send.at[p], sum_recv.at[p], r, across
        ))
        sum_copies[p].start()

    inner_taps(sent[1], 1 - u, v)
    outer_taps(sent[1], 1 - u, v)
    part_copies.append(remote(
        part_ref.at[1], partin_ref.at[1], part_send.at[parts], part_recv.at[parts], r, pair
    ))
    part_copies[parts].start()
    inner_taps(acc1_ref, u, v)
    outer_taps(acc1_ref, u, v)
    part_copies[parts].wait_recv()

    user = r + jnp.where(c == 1, 1, 0) - jnp.where(c == 2, 1, 0)
    source = r - jnp.where(c == 0, 1, 0) + jnp.where(c == 3, 1, 0)
    used = jnp.logical_and(user >= 0, user < ring)
    fed = jnp.logical_and(source >= 0, source < ring)
    gathers, row_copies = [], []
    for p in range(parts):
        where = pl.ds(p * span, span)
        gathers.append(remote(
            raw_ref.at[other, v, where], raw_ref.at[v, v, where], gather_send.at[p], gather_recv.at[p], r, across
        ))
    for i, h in enumerate((v, other)):
        for p in range(parts):
            where = pl.ds(p * span, span)
            row_copies.append(remote(
                raw_ref.at[other, h, where], raw_ref.at[v, h, where],
                row_send.at[parts * i + p], row_recv.at[parts * i + p], user, pair,
            ))
    for p in range(parts):
        where = pl.ds(p * span, span)
        sum_copies[p].wait_recv()
        raw_ref[other, v, where, :] = acc1_ref[where, :] + partin_ref[1, where, :] + sumin_ref[where, :]
        gathers[p].start()
        pl.when(used)(row_copies[p].start)

    slot = 2 * r + u
    mine = raw_ref[other, v]
    stats_ref[slot] = jnp.zeros(stats_ref.shape[1:], jnp.float32)
    stats_ref[slot, 0:1, :] = jnp.sum(mine, axis=0, keepdims=True)
    stats_ref[slot, 1:2, :] = jnp.sum(mine * mine, axis=0, keepdims=True)

    def stats_copy(i):
        return remote(
            stats_ref.at[slot], stats_ref.at[slot], stats_send.at[i], stats_recv.at[slot],
            lax.div(i, 2), 2 * v + lax.rem(i, 2),
        )

    def stats_arrival(i):
        return remote(
            stats_ref.at[i], stats_ref.at[i], stats_send.at[i], stats_recv.at[i],
            lax.div(i, 2), 2 * v + lax.rem(i, 2),
        )

    @pl.loop(0, peers)
    def _(i):
        @pl.when(i != slot)
        def _():
            stats_copy(i).start()

    @pl.loop(0, peers)
    def _(i):
        @pl.when(i != slot)
        def _():
            stats_arrival(i).wait_recv()

    sums = jnp.sum(stats_ref[:, 0:2, :], axis=0)
    group = 2 * half_width // GROUPS
    line = lax.div(lax.broadcasted_iota(jnp.int32, (half_width, half_width), 0), group)
    column = lax.div(lax.broadcasted_iota(jnp.int32, (half_width, half_width), 1), group)
    members = (line == column).astype(jnp.float32)
    eight = jnp.concatenate([sums, jnp.zeros((6, half_width), jnp.float32)], axis=0)
    totals = jnp.dot(eight, members, precision=lax.Precision.HIGHEST, preferred_element_type=jnp.float32)
    mean = totals[0:1] / count
    variance = totals[1:2] / count - mean * mean
    gs_copy.wait_recv()
    gain = jnp.concatenate([gs_ref[0, 0:1, :], gs_ref[1, 0:1, :]], axis=1)
    vec_ref[v] = jnp.zeros(vec_ref.shape[1:], jnp.float32)
    vec_ref[v, 0:1, :] = mean
    vec_ref[v, 1:2, :] = gain / jnp.sqrt(variance + epsilon)
    vec_ref[v, 2:3, :] = jnp.concatenate([gs_ref[0, 1:2, :], gs_ref[1, 1:2, :]], axis=1)
    vec_copy = remote(vec_ref.at[v], vec_ref.at[v], vec_send, vec_recv, r, across)
    vec_copy.start()

    acc2_ref[...] = jnp.zeros_like(acc2_ref)
    odd = u.astype(jnp.float32)

    @pl.when(jnp.logical_not(fed))
    def _():
        raw_ref[v] = jnp.zeros(raw_ref.shape[1:], jnp.float32)

    def normalise(half):
        mean, scale, shift = (vec_ref[half, i:i + 1, :] for i in range(3))
        for row in range(2):
            keep = jnp.where(jnp.logical_or(fed, row != v), 1.0, 0.0)
            for frame in range(frames):
                value = raw_ref[row, half, frame * breadth:(frame + 1) * breadth, :]
                value = (value - mean) * scale + shift
                value = value / (1.0 + jnp.exp(-value))
                store_shifted(xc2_ref, frame, row, value * keep)

    def second_step(i):
        w2_copy(i).wait()
        w_ref = w2_ref.at[i % 2]
        t = i % 3
        for row in range(2):
            taps = []
            for col in range(3):
                middle = w_ref[3 + col]
                if row == 0:
                    taps.append(w_ref[col] + odd * middle)
                else:
                    taps.append(w_ref[6 + col] + (1.0 - odd) * middle)
            slab = xc2_ref[t:t + frames, row].reshape(frames * breadth, 6 * half_width)
            for q in range(2):
                both = [taps[0], taps[1] + taps[2]] if q == 0 else [taps[0] + taps[1], taps[2]]
                high, low = split(jnp.concatenate(both, axis=0))
                x_high = slab[:, q * half_width:(q + 2) * half_width]
                x_low = slab[:, (3 + q) * half_width:(5 + q) * half_width]
                acc2_ref[q] += dot(x_high, high) + dot(x_low, high) + dot(x_high, low)
        if i + 2 < 6:
            w2_copy(i + 2).start()

    for p in range(parts):
        pl.when(fed)(row_copies[p].wait_recv)
    normalise(v)
    second_step(0)
    for p in range(parts):
        gathers[p].wait_recv()
        pl.when(used)(row_copies[parts + p].start)
        second_step(1 + p)
    vec_copy.wait_recv()
    for p in range(parts):
        pl.when(fed)(row_copies[parts + p].wait_recv)
    normalise(other)
    for i in range(3, 6):
        second_step(i)

    lanes = out_ref.shape[3] // 128
    for frame in range(frames):
        for q in range(2):
            rows = acc2_ref[q, frame * breadth:(frame + 1) * breadth, :] + bias_ref[...]
            for lane in range(lanes):
                mix_ref[lane, pl.ds(q, breadth, stride=2), :] = rows[:, lane * 128:(lane + 1) * 128]
        for lane in range(lanes):
            out_ref[frame, 0, :, lane * 128:(lane + 1) * 128] = mix_ref[lane]

    for p in range(parts):
        pl.when(down)(halo_down[p].wait_send)
        pl.when(up)(halo_up[p].wait_send)
    gs_copy.wait_send()
    vec_copy.wait_send()
    for copy in part_copies + sum_copies + gathers:
        copy.wait_send()

    @pl.when(used)
    def _():
        for copy in row_copies:
            copy.wait_send()

    @pl.loop(0, peers)
    def _(i):
        @pl.when(i != slot)
        def _():
            stats_copy(i).wait_send()


def shards(latent, first_weight, norm_gain, norm_shift, second_weight, out_bias):
    frames, height, breadth, inner = latent.shape
    channels = first_weight.shape[-1]
    outer = second_weight.shape[-1]
    ring = lax.axis_size("rows")
    half = channels // 2
    pixels = frames * breadth
    count = float(frames * height * ring * breadth * (channels // GROUPS))
    f32, b16 = jnp.float32, jnp.bfloat16
    dma = pltpu.SemaphoreType.DMA
    vmem = pl.BlockSpec(memory_space=pltpu.VMEM)
    hbm = pl.BlockSpec(memory_space=pl.ANY)
    return pl.pallas_call(
        functools.partial(block_kernel, ring, count),
        out_shape=jax.ShapeDtypeStruct((frames, 1, 2 * breadth, outer), f32),
        in_specs=[vmem, vmem, vmem, vmem, hbm, hbm],
        out_specs=vmem,
        scratch_shapes=[
            pltpu.VMEM(first_weight.shape, f32),
            pltpu.VMEM((2, 9, 3 * inner, half), b16),
            pltpu.VMEM((2, 9, 3 * inner, half), b16),
            pltpu.VMEM((2, frames, 1, breadth, inner), f32),
            pltpu.VMEM((frames + 2, height + 2, breadth, 6 * inner), b16),
            pltpu.VMEM((pixels, half), f32),
            pltpu.VMEM((2, pixels, half), f32),
            pltpu.VMEM((2, pixels, half), f32),
            pltpu.VMEM((pixels, half), f32),
            pltpu.VMEM((pixels, half), f32),
            pltpu.VMEM((2, 2, pixels, half), f32),
            pltpu.VMEM((2 * ring, 8, half), f32),
            pltpu.VMEM((2, 8, half), f32),
            pltpu.VMEM((2, 8, inner), f32),
            pltpu.VMEM((2, 9, half, outer), f32),
            pltpu.VMEM((frames + 2, 2, breadth, 6 * half), b16),
            pltpu.VMEM((2, pixels, outer), f32),
            pltpu.VMEM((outer // 128, 2 * breadth, 128), f32),
            dma((3,)), dma((2,)), dma((4,)), dma((4,)), dma, dma, dma((3,)), dma((3,)),
            dma((2,)), dma((2,)), dma((2 * ring,)), dma((2 * ring,)), dma((2,)), dma((2,)),
            dma((4,)), dma((4,)), dma, dma,
        ],
        compiler_params=pltpu.CompilerParams(
            collective_id=0, has_side_effects=True, vmem_limit_bytes=VMEM_LIMIT
        ),
    )(
        latent, norm_gain.reshape(1, inner), norm_shift.reshape(1, inner), out_bias.reshape(1, outer),
        first_weight, second_weight,
    )


def solution(mesh):
    return jax.shard_map(
        shards,
        mesh=mesh,
        in_specs=(P(None, "rows", None, "ch"), P(None, "ch", None), P("ch"), P("ch"), P(), P()),
        out_specs=P(None, ("rows", "ch"), None, None),
        check_vma=False,
    )
```
